32 devices in a mesh: batch: 8 (over y, x, core), blk: 4 (over z).
Axes of the slice: x: 2, y: 2, z: 4, core: 2. Of those that a mesh axis runs over, the one named last changes fastest.
Arguments:
- hidden_in: bfloat16 [64, 512, 768], P('batch', 'blk'), may hold values from -6 to 6
- lengths: int32 [64, 8], P('batch'), may hold values from 0 to 512, as said below
- qkv_weight: bfloat16 [768, 2304], replicated, may hold values from -0.21875 to 0.21875
- qv_bias: bfloat16 [2, 768], replicated, may hold values from -3 to 3
- out_weight: bfloat16 [768, 768], replicated, may hold values from -0.875 to 0.875
- out_bias: bfloat16 [768], replicated, may hold values from -2 to 2
- attn_gain: bfloat16 [768], replicated, may hold values from 0.5 to 1.5
- attn_shift: bfloat16 [768], replicated, may hold values from -2 to 2
- up_weight: bfloat16 [768, 3072], replicated, may hold values from -0.21875 to 0.21875
- up_bias: bfloat16 [3072], replicated, may hold values from -3 to 3
- down_weight: bfloat16 [3072, 768], replicated, may hold values from -0.109375 to 0.109375
- down_bias: bfloat16 [768], replicated, may hold values from -2 to 2
- ffn_gain: bfloat16 [768], replicated, may hold values from 0.5 to 1.5
- ffn_shift: bfloat16 [768], replicated, may hold values from -2 to 2
- head_weight: bfloat16 [768], replicated, may hold values from -0.21875 to 0.21875
- head_bias: bfloat16 [1], replicated, may hold values from -3 to 3
- hidden_cot: bfloat16 [64, 512, 768], P('batch', 'blk'), may hold values from -6 to 6
- term_cot: float32 [64, 512], P('batch', 'blk'), may hold values from -6 to 6
Outputs:
- hidden_out: bfloat16 [64, 512, 768], P('batch', 'blk')
- term_weight: float32 [64, 512], P('batch', 'blk')
- grad_hidden: float32 [64, 512, 768], P('batch', 'blk')
- grad_qkv_weight: float32 [768, 2304], replicated
- grad_qv_bias: float32 [2, 768], replicated
- grad_out_weight: float32 [768, 768], replicated
- grad_out_bias: float32 [768], replicated
- grad_attn_gain: float32 [768], replicated
- grad_attn_shift: float32 [768], replicated
- grad_up_weight: float32 [768, 3072], replicated
- grad_up_bias: float32 [3072], replicated
- grad_down_weight: float32 [3072, 768], replicated
- grad_down_bias: float32 [768], replicated
- grad_ffn_gain: float32 [768], replicated
- grad_ffn_shift: float32 [768], replicated
- grad_head_weight: float32 [768], replicated
- grad_head_bias: float32 [1], replicated
The draws below stay inside these ranges and needn't reach their ends.
Inputs may be any that keep to these rules, and one draw needn't show every extreme that they name: Row r of lengths holds, in order, the token counts of the passages packed into row r from its first slot on; they add up to 512 or less, and the remaining slots are padding.
All inputs are finite; a program needn't handle non-finite values.
Results may differ from the reference program's by a relative error of at most 0.018.
Values may be sent and summed in bfloat16 or wider, within the bound.
No kernel may reach another device: no remote copies, remote signals or barrier semaphores. Data moves between devices by JAX's collectives and lax.ppermute only.
A program may use at most 256 MiB of HBM per device.

```python
import jax
import jax.numpy as jnp
from jax import lax

D = 768
HEADS = 12
HD = 64
FF = 3072
ROWS_DEV = 8
SLOTS = 512
PASS = 8
ROWS = 64


def draw_lengths(key, part):
    key = jax.random.fold_in(key, 17)
    sub_keys = jax.random.split(key, 5)
    fill_len = jax.random.randint(sub_keys[0], (ROWS,), SLOTS // 2, SLOTS + 1)
    powers = jax.random.randint(sub_keys[1], (ROWS, PASS), 0, 6)
    base_len = jax.random.randint(sub_keys[2], (ROWS, PASS), 1, 9)
    raw_len = jnp.left_shift(base_len, powers) * SLOTS // 512 + 1
    chosen = jax.random.randint(sub_keys[3], (ROWS // ROWS_DEV,), 0, ROWS_DEV)
    row_index = jnp.arange(ROWS, dtype=jnp.int32)
    is_long = row_index % ROWS_DEV == jnp.repeat(chosen, ROWS_DEV)
    long_len = jax.random.randint(sub_keys[4], (ROWS,), 3 * SLOTS // 4 + 1, SLOTS + 1)
    long_len = jnp.where(row_index < ROWS_DEV, SLOTS, long_len)
    raw_len = raw_len.at[:, 0].set(jnp.where(is_long, long_len, raw_len[:, 0]))
    fill_len = jnp.where(is_long, jnp.maximum(fill_len, long_len), fill_len)
    passage_ends = jnp.minimum(jnp.cumsum(raw_len, axis=1), fill_len[:, None])
    starts = jnp.concatenate([jnp.zeros((ROWS, 1), jnp.int32), passage_ends[:, :-1]], axis=1)
    return (passage_ends - starts).astype(jnp.int32)


def levels(key, shape, shards, low, top_value):
    level, own = 1.0, jax.random.fold_in(key, 6)
    for position, parts in shards:
        draws = jnp.exp(jax.random.uniform(jax.random.fold_in(own, position), (parts,), jnp.float32, low / len(shards), top_value / len(shards)))
        level = level * jnp.repeat(draws, shape[position] // parts).reshape([-1 if axis == position else 1 for axis in range(len(shape))])
    return level


def scatter_about(key, dims, spread, limit, cuts=(), kind=jnp.bfloat16):
    level = levels(key, dims, cuts, -0.22, 0.18) if cuts else 1.0
    array = jax.random.normal(key, dims, jnp.float32) * spread * level
    return jnp.minimum(jnp.maximum(array, -limit), limit).astype(kind)


def setup_inputs(seed: int = 0) -> dict:
    streams_of = jax.random.split(jax.random.key(seed), 19)
    hidden_in = scatter_about(streams_of[0], (ROWS, SLOTS, D), 1.0, 6.0, ((0, 8), (1, 4)))
    lengths = draw_lengths(jax.random.fold_in(streams_of[18], 71), 0)
    qkv_weight = scatter_about(streams_of[2], (D, 3 * D), D ** -0.5, 0.21875)
    qv_bias = scatter_about(streams_of[3], (2, D), 0.5, 3.0)
    out_weight = scatter_about(streams_of[4], (D, D), (D // 16) ** -0.5, 0.875)
    out_bias = scatter_about(streams_of[5], (D,), 0.3, 2.0)
    attn_gain = jnp.clip(1.0 + 0.1 * jax.random.normal(streams_of[6], (D,), jnp.float32), 0.5, 1.5).astype(jnp.bfloat16)
    attn_shift = scatter_about(streams_of[7], (D,), 0.3, 2.0)
    up_weight = scatter_about(streams_of[8], (D, FF), D ** -0.5, 0.21875)
    up_bias = scatter_about(streams_of[9], (FF,), 0.5, 3.0)
    down_weight = scatter_about(streams_of[10], (FF, D), FF ** -0.5, 0.109375)
    down_bias = scatter_about(streams_of[11], (D,), 0.3, 2.0)
    ffn_gain = jnp.clip(1.0 + 0.1 * jax.random.normal(streams_of[12], (D,), jnp.float32), 0.5, 1.5).astype(jnp.bfloat16)
    ffn_shift = scatter_about(streams_of[13], (D,), 0.3, 2.0)
    head_weight = scatter_about(streams_of[14], (D,), D ** -0.5, 0.21875)
    head_bias = scatter_about(streams_of[15], (1,), 1.0, 3.0)
    hidden_cot = scatter_about(streams_of[16], (ROWS, SLOTS, D), 1.0, 6.0, ((0, 8), (1, 4)))
    term_cot = scatter_about(streams_of[17], (ROWS, SLOTS), 1.0, 6.0, ((0, 8), (1, 4)), jnp.float32)
    return {"hidden_in": hidden_in, "lengths": lengths, "qkv_weight": qkv_weight, "qv_bias": qv_bias, "out_weight": out_weight, "out_bias": out_bias, "attn_gain": attn_gain, "attn_shift": attn_shift, "up_weight": up_weight, "up_bias": up_bias, "down_weight": down_weight, "down_bias": down_bias, "ffn_gain": ffn_gain, "ffn_shift": ffn_shift, "head_weight": head_weight, "head_bias": head_bias, "hidden_cot": hidden_cot, "term_cot": term_cot}


@jax.custom_vjp
def low(v):
    return lax.optimization_barrier(v.astype(jnp.bfloat16)).astype(jnp.float32)

@jax.custom_vjp
def low_back(v):
    return v

def low_keep(v):
    return (low(v), None)

def low_pass(kept, grad):
    return (grad,)

def back_keep(v):
    return (v, None)

def back_low(kept, grad):
    return (low(grad),)
low.defvjp(low_keep, low_pass)
low_back.defvjp(back_keep, back_low)
epsilon = 1e-06
masked_score = -1e+30

def matmul(left, right):
    return jnp.dot(left, right, precision=lax.Precision.HIGHEST, preferred_element_type=jnp.float32)

def layer_norm(values, norm_gain, norm_shift):
    center = values - lax.optimization_barrier(jnp.mean(values, axis=-1, keepdims=True))
    variance = lax.optimization_barrier(jnp.mean(center * center, axis=-1, keepdims=True))
    return center * lax.rsqrt(variance + epsilon) * norm_gain + norm_shift

def gelu_exact(values):
    return jax.nn.gelu(values, approximate=False)

def document_ids(lengths, slot_count):
    passage_ends = jnp.cumsum(lengths, axis=-1)
    slot_index = jnp.arange(slot_count, dtype=jnp.int32)
    return lax.optimization_barrier(jnp.sum((passage_ends[..., None, :] <= slot_index[:, None]).astype(jnp.int32), axis=-1))

def layer_row(row_tokens, row_doc, params):
    qkv_weight, qv_bias, out_weight, out_bias, attn_gain, attn_shift, up_weight, up_bias, down_weight, down_bias, ffn_gain, ffn_shift, head_weight, head_bias = params
    model_width = row_tokens.shape[-1]
    qkv_add = jnp.concatenate([qv_bias[0], jnp.zeros_like(qv_bias[0]), qv_bias[1]])
    projected = low_back(low(matmul(row_tokens, qkv_weight) + qkv_add))
    queries = projected[:, :model_width].reshape(SLOTS, HEADS, HD)
    keys_part = projected[:, model_width:2 * model_width].reshape(SLOTS, HEADS, HD)
    vals_part = projected[:, 2 * model_width:].reshape(SLOTS, HEADS, HD)
    scores = jnp.einsum('qhd,khd->hqk', queries, keys_part, precision=lax.Precision.HIGHEST) * HD ** (-0.5)
    scores = low_back(scores)
    same_doc = row_doc[:, None] == row_doc[None, :]
    scores = jnp.where(same_doc[None], scores, masked_score)
    row_max = lax.optimization_barrier(jnp.max(scores, axis=-1, keepdims=True))
    weights = jnp.exp(scores - row_max)
    probs_low = low(weights / lax.optimization_barrier(jnp.sum(weights, axis=-1, keepdims=True)))
    mixed = jnp.einsum('hqk,khd->qhd', probs_low, vals_part, precision=lax.Precision.HIGHEST)
    attended = low_back(low(mixed.reshape(SLOTS, model_width)))
    attn_add = low_back(matmul(attended, out_weight) + out_bias)
    normed = layer_norm(row_tokens + attn_add, attn_gain, attn_shift)
    gate_pre = low_back(matmul(low(normed), up_weight) + up_bias)
    activated = low(gelu_exact(gate_pre))
    ffn_add = low_back(matmul(activated, down_weight) + down_bias)
    final_out = layer_norm(normed + ffn_add, ffn_gain, ffn_shift)
    logits = matmul(final_out, head_weight[:, None])[:, 0] + head_bias[0]
    return (final_out, jax.nn.softplus(logits))

def reference(hidden_in, lengths, qkv_weight, qv_bias, out_weight, out_bias, attn_gain, attn_shift, up_weight, up_bias, down_weight, down_bias, ffn_gain, ffn_shift, head_weight, head_bias, hidden_cot, term_cot):
    docs = document_ids(lengths, SLOTS)
    params = (qkv_weight.astype(jnp.float32), qv_bias.astype(jnp.float32), out_weight.astype(jnp.float32), out_bias.astype(jnp.float32), attn_gain.astype(jnp.float32), attn_shift.astype(jnp.float32), up_weight.astype(jnp.float32), up_bias.astype(jnp.float32), down_weight.astype(jnp.float32), down_bias.astype(jnp.float32), ffn_gain.astype(jnp.float32), ffn_shift.astype(jnp.float32), head_weight.astype(jnp.float32), head_bias.astype(jnp.float32))

    def whole(tokens, weights):

        def one_row(pieces):
            return layer_row(pieces[0], pieces[1], weights)
        return lax.map(jax.checkpoint(one_row), (tokens, docs))
    (final_out, term_weight), pullback = jax.vjp(whole, hidden_in.astype(jnp.float32), params)
    grad_hidden, grads = pullback((hidden_cot.astype(jnp.float32), term_cot))
    return (final_out.astype(jnp.bfloat16), term_weight, grad_hidden, grads[0], grads[1], grads[2], grads[3], grads[4], grads[5], grads[6], grads[7], grads[8], grads[9], grads[10], grads[11], grads[12], grads[13])
```

```python
import jax
import jax.numpy as jnp
from jax import lax
from jax.sharding import PartitionSpec as P

HEADS = 12
HD = 64


epsilon = 1e-06
masked_score = -1e30


def layer_norm(values, norm_gain, norm_shift):
    center = values - jnp.mean(values, axis=-1, keepdims=True)
    variance = jnp.mean(center * center, axis=-1, keepdims=True)
    return center * lax.rsqrt(variance + epsilon) * norm_gain + norm_shift


def norm_backward(values, norm_gain, norm_shift, upstream):
    result, pullback = jax.vjp(layer_norm, values, norm_gain, norm_shift)
    return pullback(upstream)


def gelu_exact(values):
    return jax.nn.gelu(values, approximate=False)


def document_ids(lengths, slot_count):
    passage_ends = jnp.cumsum(lengths, axis=-1)
    slot_index = jnp.arange(slot_count, dtype=jnp.int32)
    return jnp.sum((passage_ends[..., None, :] <= slot_index[:, None]).astype(jnp.int32), axis=-1)


AXES = ("batch", "blk")


def bits_of(count):
    return max(count - 1, 0).bit_length()


def is_power(count):
    return count & (count - 1) == 0


def flat_perm(sizes, partner):
    pairs = []
    for b in range(sizes[0]):
        for z in range(sizes[1]):
            to_b, to_z = partner(b, z)
            pairs.append((b * sizes[1] + z, to_b * sizes[1] + to_z))
    return pairs


def move(array, sizes, partner):
    return lax.ppermute(array, AXES, flat_perm(sizes, partner))


def segment_exchange(blocks, sizes):
    nz = sizes[1]
    return [blocks[0]] + [
        move(blocks[k], sizes, lambda b, z, k=k: (b, (z + k) % nz)) for k in range(1, nz)
    ]


def segment_return(blocks, sizes):
    nz = sizes[1]
    return [blocks[0]] + [
        move(blocks[k], sizes, lambda b, z, k=k: (b, (z - k) % nz)) for k in range(1, nz)
    ]


def to_rows(local, sizes):
    nz = sizes[1]
    z = lax.axis_index("blk")
    parts = local.reshape((nz, local.shape[0] // nz) + local.shape[1:])
    blocks = [lax.dynamic_index_in_dim(parts, (z + k) % nz, 0, False) for k in range(nz)]
    return jnp.stack(segment_exchange(blocks, sizes), axis=1)


def to_segments(rows, sizes):
    nz = sizes[1]
    z = lax.axis_index("blk")
    blocks = segment_return([rows[:, k] for k in range(nz)], sizes)
    out = jnp.zeros((nz,) + blocks[0].shape, rows.dtype)
    for k in range(nz):
        out = lax.dynamic_update_index_in_dim(out, blocks[k], (z + k) % nz, 0)
    return out.reshape((nz * rows.shape[0],) + rows.shape[2:])


def halving_steps(sizes):
    batch_bits, blk_bits = bits_of(sizes[0]), bits_of(sizes[1])
    middle = list(range(1, batch_bits))
    forward = [("b", 0)] if batch_bits else []
    steps = [(step, step) for step in forward]
    steps += [(("b", p), ("b", q)) for p, q in zip(middle, reversed(middle))]
    steps += [(("z", p), ("z", p)) for p in range(blk_bits)]
    return steps


def step_partner(step):
    def partner(b, z):
        axis, bit = step[b & 1]
        return (b ^ (1 << bit), z) if axis == "b" else (b, z ^ (1 << bit))

    return partner


def own_bit(step):
    b, z = lax.axis_index("batch"), lax.axis_index("blk")

    def value(part):
        return ((b if part[0] == "b" else z) >> part[1]) & 1

    return jnp.where(b & 1 == 1, value(step[1]), value(step[0]))


def sum_all(array, sizes):
    steps = halving_steps(sizes)
    part = array.astype(jnp.bfloat16)
    for step in steps:
        bit = own_bit(step)
        halves = part.reshape((2, part.shape[0] // 2) + part.shape[1:])
        keep = lax.dynamic_index_in_dim(halves, bit, 0, False)
        send = lax.dynamic_index_in_dim(halves, 1 - bit, 0, False)
        got = move(send, sizes, step_partner(step))
        part = (keep.astype(jnp.float32) + got.astype(jnp.float32)).astype(jnp.bfloat16)
    for step in reversed(steps):
        bit = own_bit(step)
        got = move(part, sizes, step_partner(step))
        low = jnp.where(bit == 0, part, got)
        high = jnp.where(bit == 0, got, part)
        part = jnp.concatenate([low, high], axis=0)
    return part.astype(jnp.float32)


def sum_small(array, sizes):
    for step in halving_steps(sizes):
        array = array + move(array, sizes, step_partner(step))
    return array


def per_device(
    hidden_in,
    lengths,
    qkv_weight,
    qv_bias,
    out_weight,
    out_bias,
    attn_gain,
    attn_shift,
    up_weight,
    up_bias,
    down_weight,
    down_bias,
    ffn_gain,
    ffn_shift,
    head_weight,
    head_bias,
    hidden_cot,
    term_cot,
):
    row_count, seg_len, model_width = hidden_in.shape
    sizes = (lax.axis_size("batch"), lax.axis_size("blk"))
    nz = sizes[1]
    own_rows = row_count // nz
    slot_count = seg_len * nz
    score_scale = HD ** (-0.5)
    blk_index = lax.axis_index("blk")
    doc_all = document_ids(lengths, slot_count)
    doc_mine = lax.dynamic_slice_in_dim(doc_all, blk_index * own_rows, own_rows, 0)
    doc_mine = doc_mine.reshape(own_rows, nz, seg_len)
    docs = jnp.stack(
        [
            lax.dynamic_index_in_dim(doc_mine, (blk_index - k) % nz, 1, False)
            for k in range(nz)
        ],
        axis=1,
    ).reshape(own_rows, slot_count)
    token_count = own_rows * slot_count
    same_doc = (docs[:, :, None] == docs[:, None, :])[:, None]
    tokens = to_rows(hidden_in, sizes).reshape(token_count, model_width)
    cot = to_rows(hidden_cot, sizes).reshape(token_count, model_width)
    term_cot_rows = to_rows(term_cot, sizes).reshape(token_count)

    bias_query = qv_bias[0].astype(jnp.float32)
    qkv_add = jnp.concatenate(
        [bias_query, jnp.zeros_like(bias_query), qv_bias[1].astype(jnp.float32)]
    )
    projected = (jnp.dot(tokens, qkv_weight, preferred_element_type=jnp.float32) + qkv_add).astype(
        jnp.bfloat16
    )
    heads = projected.reshape(own_rows, slot_count, 3, HEADS, HD)
    queries, keys_part, vals_part = heads[:, :, 0], heads[:, :, 1], heads[:, :, 2]
    scores = (
        jnp.einsum("rqhd,rkhd->rhqk", queries, keys_part, preferred_element_type=jnp.float32)
        * score_scale
    )
    scores = jnp.where(same_doc, scores, masked_score)
    row_max = jnp.max(scores, axis=-1, keepdims=True)
    weights = jnp.exp(scores - row_max)
    row_total = jnp.sum(weights, axis=-1, keepdims=True)
    probs_low = (weights / row_total).astype(jnp.bfloat16)
    mixed = jnp.einsum("rhqk,rkhd->rqhd", probs_low, vals_part, preferred_element_type=jnp.float32)
    attended = mixed.reshape(token_count, model_width).astype(jnp.bfloat16)
    gain_attn = attn_gain.astype(jnp.float32)
    shift_attn = attn_shift.astype(jnp.float32)
    gain_ffn = ffn_gain.astype(jnp.float32)
    shift_ffn = ffn_shift.astype(jnp.float32)
    first_sum = (
        tokens.astype(jnp.float32)
        + jnp.dot(attended, out_weight, preferred_element_type=jnp.float32)
        + out_bias.astype(jnp.float32)
    )
    normed = layer_norm(first_sum, gain_attn, shift_attn)
    normed_low = normed.astype(jnp.bfloat16)
    gate_pre = jnp.dot(normed_low, up_weight, preferred_element_type=jnp.float32) + up_bias.astype(
        jnp.float32
    )
    activated = gelu_exact(gate_pre).astype(jnp.bfloat16)
    second_sum = (
        normed
        + jnp.dot(activated, down_weight, preferred_element_type=jnp.float32)
        + down_bias.astype(jnp.float32)
    )
    final_out = layer_norm(second_sum, gain_ffn, shift_ffn)
    head_vec = head_weight.astype(jnp.float32)
    logits = (
        jnp.dot(final_out, head_vec, precision=lax.Precision.HIGHEST)
        + head_bias.astype(jnp.float32)[0]
    )
    term_weight = jax.nn.softplus(logits)
    term_grad = term_cot_rows * jax.nn.sigmoid(logits)
    grad_head_weight = jnp.dot(term_grad, final_out, precision=lax.Precision.HIGHEST)
    grad_head_bias = jnp.sum(term_grad, keepdims=True)
    final_grad = (
        cot.astype(jnp.float32)
        + term_grad[:, None] * head_vec
    )
    second_grad, grad_ffn_gain, grad_ffn_shift = norm_backward(
        second_sum, gain_ffn, shift_ffn, final_grad
    )
    ffn_grad = second_grad.astype(jnp.bfloat16)
    grad_down_bias = jnp.sum(ffn_grad, axis=0, dtype=jnp.float32)
    grad_down_weight = jnp.einsum(
        "tf,td->fd", activated, ffn_grad, preferred_element_type=jnp.float32
    )
    act_grad = jnp.einsum("td,fd->tf", ffn_grad, down_weight, preferred_element_type=jnp.float32)
    gelu_pull = jax.vjp(gelu_exact, gate_pre)[1]
    gate_grad = gelu_pull(act_grad)[0].astype(jnp.bfloat16)
    grad_up_bias = jnp.sum(gate_grad, axis=0, dtype=jnp.float32)
    grad_up_weight = jnp.einsum(
        "td,tf->df", normed_low, gate_grad, preferred_element_type=jnp.float32
    )
    normed_grad = (
        jnp.einsum("tf,df->td", gate_grad, up_weight, preferred_element_type=jnp.float32)
        + second_grad
    )
    first_grad, grad_attn_gain, grad_attn_shift = norm_backward(
        first_sum, gain_attn, shift_attn, normed_grad
    )
    attn_grad = first_grad.astype(jnp.bfloat16)
    grad_out_bias = jnp.sum(attn_grad, axis=0, dtype=jnp.float32)
    grad_out_weight = jnp.einsum(
        "td,te->de", attended, attn_grad, preferred_element_type=jnp.float32
    )
    mixed_grad = jnp.einsum(
        "te,de->td", attn_grad, out_weight, preferred_element_type=jnp.float32
    ).astype(jnp.bfloat16)
    upstream = mixed_grad.reshape(own_rows, slot_count, HEADS, HD)
    dprobs = jnp.einsum("rqhd,rkhd->rhqk", upstream, vals_part, preferred_element_type=jnp.float32)
    vals_grad = jnp.einsum(
        "rhqk,rqhd->rkhd", probs_low, upstream, preferred_element_type=jnp.float32
    )
    probs = probs_low.astype(jnp.float32)
    inner_sum = jnp.sum(probs * dprobs, axis=-1, keepdims=True)
    score_grad = (probs * (dprobs - inner_sum)).astype(jnp.bfloat16)
    query_grad = (
        jnp.einsum("rhqk,rkhd->rqhd", score_grad, keys_part, preferred_element_type=jnp.float32)
        * score_scale
    )
    key_grad = (
        jnp.einsum("rhqk,rqhd->rkhd", score_grad, queries, preferred_element_type=jnp.float32)
        * score_scale
    )
    proj_grad = (
        jnp.stack([query_grad, key_grad, vals_grad], axis=2)
        .reshape(token_count, 3 * model_width)
        .astype(jnp.bfloat16)
    )
    grad_qv_bias = jnp.stack(
        [
            jnp.sum(proj_grad[:, :model_width], axis=0, dtype=jnp.float32),
            jnp.sum(proj_grad[:, 2 * model_width :], axis=0, dtype=jnp.float32),
        ]
    )
    grad_qkv_weight = jnp.einsum("td,te->de", tokens, proj_grad, preferred_element_type=jnp.float32)
    grad_hidden = (
        jnp.einsum("te,de->td", proj_grad, qkv_weight, preferred_element_type=jnp.float32)
        + first_grad
    )
    vectors = (
        grad_qv_bias,
        grad_out_bias,
        grad_attn_gain,
        grad_attn_shift,
        grad_up_bias,
        grad_down_bias,
        grad_ffn_gain,
        grad_ffn_shift,
        grad_head_weight,
        grad_head_bias,
    )
    packed = jnp.concatenate([v.reshape(-1) for v in vectors])
    packed = jnp.pad(packed, (0, -packed.size % 1024)).reshape(-1, 128)
    packed = sum_small(packed, sizes).reshape(-1)
    summed, offset = [], 0
    for v in vectors:
        summed.append(packed[offset : offset + v.size].reshape(v.shape))
        offset += v.size
    vectors = summed
    matrices = [
        sum_all(g, sizes)
        for g in (grad_down_weight, grad_up_weight, grad_out_weight, grad_qkv_weight)
    ][::-1]
    shape4 = (own_rows, nz, seg_len, model_width)
    return (
        to_segments(final_out.astype(jnp.bfloat16).reshape(shape4), sizes),
        to_segments(term_weight.reshape(shape4[:3]), sizes),
        to_segments(grad_hidden.astype(jnp.bfloat16).reshape(shape4), sizes).astype(jnp.float32),
        matrices[0],
        vectors[0],
        matrices[1],
        vectors[1],
        vectors[2],
        vectors[3],
        matrices[2],
        vectors[4],
        matrices[3],
        vectors[5],
        vectors[6],
        vectors[7],
        vectors[8],
        vectors[9],
    )


def solution(mesh):
    return jax.shard_map(
        per_device,
        mesh=mesh,
        in_specs=(
            P("batch", "blk", None),
            P("batch", None),
            P(),
            P(),
            P(),
            P(),
            P(),
            P(),
            P(),
            P(),
            P(),
            P(),
            P(),
            P(),
            P(),
            P(),
            P("batch", "blk", None),
            P("batch", "blk"),
        ),
        out_specs=(
            P("batch", "blk", None),
            P("batch", "blk"),
            P("batch", "blk", None),
            P(),
            P(),
            P(),
            P(),
            P(),
            P(),
            P(),
            P(),
            P(),
            P(),
            P(),
            P(),
            P(),
            P(),
        ),
        check_vma=False,
    )
```

```python
import functools

import jax
import jax.numpy as jnp
from jax import lax
from jax.experimental import pallas as pl
from jax.experimental.pallas import tpu as pltpu
from jax.sharding import PartitionSpec as P

HD = 64
AXES = ("batch", "blk")
epsilon = 1e-06
masked_score = -1e30
f32 = jnp.float32
bf16 = jnp.bfloat16
NT = (((1,), (1,)), ((), ()))
TN = (((0,), (0,)), ((), ()))

(
    V_QUERY,
    V_VALUE,
    V_OUT,
    V_GAIN1,
    V_SHIFT1,
    V_DOWN,
    V_GAIN2,
    V_SHIFT2,
    V_HEAD,
    V_HEAD_BIAS,
    V_UP,
) = range(11)


def dot(left, right, dims=None):
    if dims is None:
        return jnp.dot(left, right, preferred_element_type=f32)
    return lax.dot_general(left, right, dims, preferred_element_type=f32)


def call_params(mebibytes):
    return pltpu.CompilerParams(vmem_limit_bytes=mebibytes * 2**20)


def cost(flops, arrays):
    moved = sum(a.size * a.dtype.itemsize for a in arrays)
    return pl.CostEstimate(flops=int(flops), bytes_accessed=int(moved), transcendentals=0)


def whole(array, buffers=None):
    spec = {} if buffers is None else {"pipeline_mode": pl.Buffered(buffers)}
    return pl.BlockSpec(array.shape, lambda *i: (0,) * array.ndim, **spec)


def column_sum(values):
    return jnp.sum(values, axis=0, keepdims=True)


def row_mean(values):
    return jnp.mean(values, axis=-1, keepdims=True)


def to_column(row, count):
    return jnp.transpose(jnp.broadcast_to(row, (128, count)))[:, 0:1]


def to_row(column, count):
    return jnp.transpose(jnp.broadcast_to(column, (count, 128)))[0:1, :]


def attend_kernel(
    nz, own_rows, row, lengths, x_ref, wq, wk, wv, vec, q_ref, k_ref, v_ref, att_ref, p_ref, bias
):
    seg_len = x_ref.shape[0] // nz

    @pl.when(pl.program_id(0) == 0)
    def _():
        z = lax.axis_index("blk")
        mine = z * own_rows + row
        cols, rows = [], []
        for k in range(nz):
            base = lax.rem(z + (nz - k), nz) * seg_len
            col = lax.broadcasted_iota(jnp.int32, (seg_len, 1), 0) + base
            lane = lax.broadcasted_iota(jnp.int32, (1, seg_len), 1) + base
            end = jnp.int32(0)
            doc_col, doc_row = jnp.zeros_like(col), jnp.zeros_like(lane)
            for p in range(lengths.shape[1]):
                end = end + lengths[mine, p]
                doc_col += (col >= end).astype(jnp.int32)
                doc_row += (lane >= end).astype(jnp.int32)
            cols.append(doc_col)
            rows.append(doc_row)
        for i in range(nz):
            for j in range(nz):
                bias[pl.ds(i * seg_len, seg_len), pl.ds(j * seg_len, seg_len)] = jnp.where(
                    cols[i] == rows[j], 0.0, masked_score
                ).astype(f32)

    x = x_ref[...]
    q_ref[...] = (dot(x, wq[...]) + vec[V_QUERY : V_QUERY + 1, :]).astype(bf16)
    k_ref[...] = dot(x, wk[...]).astype(bf16)
    v_ref[...] = (dot(x, wv[...]) + vec[V_VALUE : V_VALUE + 1, :]).astype(bf16)
    first = lax.broadcasted_iota(jnp.int32, (1, 2 * HD), 1) < HD
    for pair in range(q_ref.shape[1] // (2 * HD)):
        cols = pl.ds(pair * 2 * HD, 2 * HD)
        q, k, v = q_ref[:, cols], k_ref[:, cols], v_ref[:, cols]
        outs = []
        for h in range(2):
            mine = first if h == 0 else jnp.logical_not(first)
            scaled = jnp.where(mine, q * jnp.asarray(HD**-0.5, bf16), jnp.zeros_like(q))
            scores = dot(scaled, k, NT) + bias[...]
            weights = jnp.exp(scores - jnp.max(scores, axis=1, keepdims=True))
            total = jnp.sum(weights, axis=1, keepdims=True)
            probs = (weights * (1.0 / total)).astype(bf16)
            p_ref[pair * 2 + h] = probs
            outs.append(dot(probs, v))
        att_ref[:, cols] = jnp.where(first, outs[0], outs[1]).astype(bf16)


def attend(x, lengths, wqkv, vec, nz, own_rows, row, width=256):
    n, d = x.shape
    steps, heads = d // width, width // HD

    def weight(part):
        return pl.BlockSpec((d, width), lambda j: (0, part * steps + j))

    token = pl.BlockSpec((n, width), lambda j: (0, j))
    return pl.pallas_call(
        functools.partial(attend_kernel, nz, own_rows, row),
        grid=(steps,),
        in_specs=[
            pl.BlockSpec(memory_space=pltpu.SMEM),
            whole(x),
            weight(0),
            weight(1),
            weight(2),
            pl.BlockSpec((vec.shape[0], width), lambda j: (0, j)),
        ],
        out_specs=[token] * 4 + [pl.BlockSpec((heads, n, n), lambda j: (j, 0, 0))],
        out_shape=[jax.ShapeDtypeStruct((n, d), bf16)] * 4
        + [jax.ShapeDtypeStruct((d // HD, n, n), bf16)],
        scratch_shapes=[pltpu.VMEM((n, n), f32)],
        compiler_params=call_params(24),
        cost_estimate=cost(12 * n * d * d, [x, wqkv]),
        name="attend",
    )(lengths, x, wqkv, wqkv, wqkv, vec)


def attend_back_kernel(
    g_ref, wo, q_ref, k_ref, v_ref, att_ref, p_ref, wq, wk, wv, dp_ref, gh_ref, sums, acc, up_s
):
    step = pl.program_id(0)
    up_s[...] = dot(g_ref[...], wo[...], NT).astype(bf16)
    first = lax.broadcasted_iota(jnp.int32, (1, 2 * HD), 1) < HD
    scale = HD**-0.5
    for pair in range(q_ref.shape[1] // (2 * HD)):
        cols = pl.ds(pair * 2 * HD, 2 * HD)
        q, k, v, up = q_ref[:, cols], k_ref[:, cols], v_ref[:, cols], up_s[:, cols]
        product = up.astype(f32) * att_ref[:, cols].astype(f32)
        dq, dk, dv = [], [], []
        for h in range(2):
            mine = first if h == 0 else jnp.logical_not(first)
            inner = jnp.sum(jnp.where(mine, product, 0.0), axis=1, keepdims=True)
            probs = p_ref[pair * 2 + h]
            dprobs = dot(jnp.where(mine, up, jnp.zeros_like(up)), v, NT)
            score_grad = (probs.astype(f32) * (dprobs - inner)).astype(bf16)
            dv.append(dot(probs, up, TN))
            dq.append(dot(score_grad, k))
            dk.append(dot(score_grad, q, TN))
        dp_ref[0, :, cols] = (jnp.where(first, dq[0], dq[1]) * scale).astype(bf16)
        dp_ref[1, :, cols] = (jnp.where(first, dk[0], dk[1]) * scale).astype(bf16)
        dp_ref[2, :, cols] = jnp.where(first, dv[0], dv[1]).astype(bf16)
    part = dot(dp_ref[0], wq[...], NT) + dot(dp_ref[1], wk[...], NT) + dot(dp_ref[2], wv[...], NT)
    sums[...] = jnp.zeros_like(sums)
    sums[0:1, :] = column_sum(dp_ref[0].astype(f32))
    sums[1:2, :] = column_sum(dp_ref[2].astype(f32))

    @pl.when(step == 0)
    def _():
        acc[...] = g_ref[...].astype(f32) + part

    @pl.when(step > 0)
    def _():
        acc[...] += part

    @pl.when(step == pl.num_programs(0) - 1)
    def _():
        gh_ref[...] = acc[...].astype(bf16)


def attend_back(g, wo, q, k, v, att, probs, wqkv, width=256):
    n, d = g.shape
    steps, heads = d // width, width // HD

    def weight(part):
        return pl.BlockSpec((d, width), lambda j: (0, part * steps + j))

    token = pl.BlockSpec((n, width), lambda j: (0, j))
    return pl.pallas_call(
        attend_back_kernel,
        grid=(steps,),
        in_specs=[
            whole(g),
            pl.BlockSpec((width, d), lambda j: (j, 0)),
            token,
            token,
            token,
            token,
            pl.BlockSpec((heads, n, n), lambda j: (j, 0, 0)),
            weight(0),
            weight(1),
            weight(2),
        ],
        out_specs=[
            pl.BlockSpec((3, n, width), lambda j: (0, 0, j)),
            whole(g),
            pl.BlockSpec((8, width), lambda j: (0, j)),
        ],
        out_shape=[
            jax.ShapeDtypeStruct((3, n, d), bf16),
            jax.ShapeDtypeStruct((n, d), bf16),
            jax.ShapeDtypeStruct((8, d), f32),
        ],
        scratch_shapes=[pltpu.VMEM((n, d), f32), pltpu.VMEM((n, width), bf16)],
        compiler_params=call_params(32),
        cost_estimate=cost(20 * n * d * d, [g, wo, q, k, v, att, probs, wqkv]),
        name="attend_back",
    )(g, wo, q, k, v, att, probs, wqkv, wqkv, wqkv)


def feed_kernel(x_ref, att_ref, wo, wu, wd, vec, hid, tw, act, slope, low, n1_ref, n2_ref, stats):
    n, d = x_ref.shape
    parts = act.shape[1] // d

    def row(i):
        return vec[i : i + 1, :]

    first_sum = x_ref[...].astype(f32) + dot(att_ref[...], wo[...]) + row(V_OUT)
    center = first_sum - row_mean(first_sum)
    scale1 = lax.rsqrt(row_mean(center * center) + epsilon)
    n1 = center * scale1
    n1_ref[...] = n1.astype(bf16)
    normed = n1 * row(V_GAIN1) + row(V_SHIFT1)
    normed_low = normed.astype(bf16)
    low[...] = normed_low
    second_sum = normed + row(V_DOWN)
    for c in range(parts):
        cols = pl.ds(c * d, d)
        gate = dot(normed_low, wu[:, cols]) + row(V_UP + c)
        below = 0.5 * (1.0 + lax.erf(gate * (0.5**0.5)))
        density = jnp.exp(-0.5 * gate * gate) * 0.3989422804014327
        active = (gate * below).astype(bf16)
        act[:, cols] = active
        slope[:, cols] = (below + gate * density).astype(bf16)
        second_sum += dot(active, wd[cols, :])
    center = second_sum - row_mean(second_sum)
    scale2 = lax.rsqrt(row_mean(center * center) + epsilon)
    n2 = center * scale2
    n2_ref[...] = n2.astype(bf16)
    final = n2 * row(V_GAIN2) + row(V_SHIFT2)
    hid[...] = final.astype(bf16)
    logits = jnp.sum(final * row(V_HEAD), axis=1, keepdims=True) + vec[V_HEAD_BIAS, 0]
    tw[...] = to_row(
        jnp.maximum(logits, 0.0) + jnp.log1p(jnp.exp(-jnp.abs(logits))), n
    )
    lane = lax.broadcasted_iota(jnp.int32, (1, 128), 1)
    stats[...] = jnp.where(lane == 0, scale1, jnp.where(lane == 1, scale2, logits))


def feed(x, att, wo, wu, wd, vec, tile):
    n, d = x.shape
    hidden = wu.shape[1]
    token = pl.BlockSpec((tile, d), lambda i: (i, 0))
    wide = pl.BlockSpec((tile, hidden), lambda i: (i, 0))
    return pl.pallas_call(
        feed_kernel,
        grid=(n // tile,),
        in_specs=[token, token, whole(wo, 1), whole(wu, 1), whole(wd, 1), whole(vec, 1)],
        out_specs=[
            token,
            pl.BlockSpec((1, tile), lambda i: (0, i)),
            wide,
            wide,
            token,
            token,
            token,
            pl.BlockSpec((tile, 128), lambda i: (i, 0)),
        ],
        out_shape=[
            jax.ShapeDtypeStruct((n, d), bf16),
            jax.ShapeDtypeStruct((1, n), f32),
            jax.ShapeDtypeStruct((n, hidden), bf16),
            jax.ShapeDtypeStruct((n, hidden), bf16),
            jax.ShapeDtypeStruct((n, d), bf16),
            jax.ShapeDtypeStruct((n, d), bf16),
            jax.ShapeDtypeStruct((n, d), bf16),
            jax.ShapeDtypeStruct((n, 128), f32),
        ],
        compiler_params=call_params(40),
        cost_estimate=cost(2 * n * d * (d + 2 * hidden), [x, att, wo, wu, wd]),
        name="feed",
    )(x, att, wo, wu, wd, vec)


def head_back_kernel(cot, term_cot, n2_ref, stats, vec, fg, sums):
    n = cot.shape[0]

    def row(i):
        return vec[i : i + 1, :]

    n2 = n2_ref[...].astype(f32)
    scale2, logits = stats[:, 1:2], stats[:, 2:3]
    term_grad = to_column(term_cot[...], n) * (1.0 / (1.0 + jnp.exp(-logits)))
    final_grad = cot[...].astype(f32) + term_grad * row(V_HEAD)
    gained = final_grad * row(V_GAIN2)
    grad = (gained - row_mean(gained) - n2 * row_mean(gained * n2)) * scale2
    grad_low = grad.astype(bf16)
    fg[...] = grad_low
    part = jnp.concatenate(
        [
            column_sum(final_grad * n2),
            column_sum(final_grad),
            column_sum(term_grad * (n2 * row(V_GAIN2) + row(V_SHIFT2))),
            column_sum(grad_low.astype(f32)),
            jnp.broadcast_to(jnp.sum(term_grad, axis=0, keepdims=True), (1, cot.shape[1])),
            jnp.zeros((3, cot.shape[1]), f32),
        ],
        axis=0,
    )

    @pl.when(pl.program_id(0) == 0)
    def _():
        sums[...] = part

    @pl.when(pl.program_id(0) > 0)
    def _():
        sums[...] += part


def head_back(cot, term_cot, n2, stats, vec, tile):
    n, d = cot.shape
    token = pl.BlockSpec((tile, d), lambda i: (i, 0))
    return pl.pallas_call(
        head_back_kernel,
        grid=(n // tile,),
        in_specs=[
            token,
            pl.BlockSpec((1, tile), lambda i: (0, i)),
            token,
            pl.BlockSpec((tile, 128), lambda i: (i, 0)),
            whole(vec, 1),
        ],
        out_specs=[token, pl.BlockSpec((8, d), lambda i: (0, 0))],
        out_shape=[jax.ShapeDtypeStruct((n, d), bf16), jax.ShapeDtypeStruct((8, d), f32)],
        compiler_params=call_params(16),
        cost_estimate=cost(20 * n * d, [cot, n2]),
        name="head_back",
    )(cot, term_cot, n2, stats, vec)


def feed_back_kernel(fg_ref, slope, n1_ref, stats, wu, wd, vec, gate_grad, ag, sums):
    d = fg_ref.shape[1]
    parts = slope.shape[1] // d
    fg = fg_ref[...]
    total = fg.astype(f32)
    ups = []
    for c in range(parts):
        cols = pl.ds(c * d, d)
        grad = (dot(fg, wd[cols, :], NT) * slope[:, cols].astype(f32)).astype(bf16)
        gate_grad[:, cols] = grad
        ups.append(column_sum(grad.astype(f32)))
        total += dot(grad, wu[:, cols], NT)
    n1 = n1_ref[...].astype(f32)
    gained = total * vec[V_GAIN1 : V_GAIN1 + 1, :]
    low = ((gained - row_mean(gained) - n1 * row_mean(gained * n1)) * stats[:, 0:1]).astype(bf16)
    ag[...] = low
    part = jnp.concatenate(
        [column_sum(total * n1), column_sum(total), column_sum(low.astype(f32))]
        + ups
        + [jnp.zeros((sums.shape[0] - 3 - parts, d), f32)],
        axis=0,
    )

    @pl.when(pl.program_id(0) == 0)
    def _():
        sums[...] = part

    @pl.when(pl.program_id(0) > 0)
    def _():
        sums[...] += part


def feed_back(fg, slope, n1, stats, wu, wd, vec, tile):
    n, d = fg.shape
    hidden = wu.shape[1]
    count = -(-(3 + hidden // d) // 8) * 8
    token = pl.BlockSpec((tile, d), lambda i: (i, 0))
    wide = pl.BlockSpec((tile, hidden), lambda i: (i, 0))
    return pl.pallas_call(
        feed_back_kernel,
        grid=(n // tile,),
        in_specs=[
            token,
            wide,
            token,
            pl.BlockSpec((tile, 128), lambda i: (i, 0)),
            whole(wu, 1),
            whole(wd, 1),
            whole(vec, 1),
        ],
        out_specs=[wide, token, pl.BlockSpec((count, d), lambda i: (0, 0))],
        out_shape=[
            jax.ShapeDtypeStruct((n, hidden), bf16),
            jax.ShapeDtypeStruct((n, d), bf16),
            jax.ShapeDtypeStruct((count, d), f32),
        ],
        compiler_params=call_params(40),
        cost_estimate=cost(4 * n * d * hidden, [fg, slope, n1, wu, wd]),
        name="feed_back",
    )(fg, slope, n1, stats, wu, wd, vec)


def weight_kernel(count, which, *refs):
    out = refs[-1]
    total = dot(refs[0][...], refs[count][...].reshape(refs[count].shape[-2:]), TN)
    for i in range(1, count):
        total += dot(refs[i][...], refs[count + i][...].reshape(refs[count].shape[-2:]), TN)
    out[...] = total.astype(bf16)


def weight_grad(lefts, rights, which, block):
    count = len(lefts)
    n, rows = lefts[0].shape
    half = rows // 2
    parts = rights[0].shape[0] if rights[0].ndim == 3 else 1
    width = rights[0].shape[-1]
    if rights[0].ndim == 3:
        grid = (parts, width // block)
        left = pl.BlockSpec((n, half), lambda p, j, w: (0, w[0]))
        right = pl.BlockSpec((1, n, block), lambda p, j, w: (p, 0, j))
        out = pl.BlockSpec((half, block), lambda p, j, w: (0, p * (width // block) + j))
    else:
        grid = (half // block,)
        left = pl.BlockSpec((n, block), lambda j, w: (0, w[0] * (half // block) + j))
        right = pl.BlockSpec((n, width), lambda j, w: (0, 0))
        out = pl.BlockSpec((block, width), lambda j, w: (j, 0))
    return pl.pallas_call(
        lambda w, *refs: weight_kernel(count, w, *refs),
        grid_spec=pltpu.PrefetchScalarGridSpec(
            num_scalar_prefetch=1,
            grid=grid,
            in_specs=[left] * count + [right] * count,
            out_specs=out,
        ),
        out_shape=jax.ShapeDtypeStruct((half, parts * width), bf16),
        compiler_params=call_params(32),
        cost_estimate=cost(2 * count * n * half * parts * width, list(rights)),
        name="weight_grad",
    )(which, *lefts, *rights)


def join_kernel(count, bit, mine, other, out):
    here = pl.program_id(0) // count == bit[0]
    out[...] = jnp.where(here, mine[...], other[...]).astype(out.dtype)


def join(mine, other, bit, dtype, block):
    rows, width = mine.shape
    count = rows // block

    def place(i, own):
        return jnp.clip(i - own * count, 0, count - 1)

    return pl.pallas_call(
        lambda b, *refs: join_kernel(count, b, *refs),
        grid_spec=pltpu.PrefetchScalarGridSpec(
            num_scalar_prefetch=1,
            grid=(2 * count,),
            in_specs=[
                pl.BlockSpec((block, width), lambda i, b: (place(i, b[0]), 0)),
                pl.BlockSpec((block, width), lambda i, b: (place(i, 1 - b[0]), 0)),
            ],
            out_specs=pl.BlockSpec((block, width), lambda i, b: (i, 0)),
        ),
        out_shape=jax.ShapeDtypeStruct((2 * rows, width), dtype),
        compiler_params=call_params(24),
        cost_estimate=cost(0, [mine, mine, mine, mine]),
        name="join",
    )(bit, mine, other)


def bits_of(count):
    return max(count - 1, 0).bit_length()


def move(array, sizes, partner):
    pairs = []
    for b in range(sizes[0]):
        for z in range(sizes[1]):
            to_b, to_z = partner(b, z)
            pairs.append((b * sizes[1] + z, to_b * sizes[1] + to_z))
    return lax.ppermute(array, AXES, pairs)


def send_round(blocks, sizes, sign):
    nz = sizes[1]
    return [blocks[0]] + [
        move(blocks[k], sizes, lambda b, z, k=k: (b, (z + sign * k) % nz)) for k in range(1, nz)
    ]


def to_rows(local, sizes, row):
    nz = sizes[1]
    z = lax.axis_index("blk")
    own_rows = local.shape[0] // nz
    blocks = [
        lax.dynamic_index_in_dim(local, ((z + k) % nz) * own_rows + row, 0, False)
        for k in range(nz)
    ]
    return send_round(blocks, sizes, 1)


def to_segments(rows, sizes):
    nz, own_rows = sizes[1], len(rows)
    z = lax.axis_index("blk")
    got = [send_round(row, sizes, -1) for row in rows]
    out = jnp.zeros((nz * own_rows,) + got[0][0].shape, got[0][0].dtype)
    for k in range(nz):
        for r in range(own_rows):
            out = lax.dynamic_update_index_in_dim(out, got[r][k], ((z + k) % nz) * own_rows + r, 0)
    return out


def halving_steps(sizes):
    batch_bits, blk_bits = bits_of(sizes[0]), bits_of(sizes[1])
    middle = [("b", bit) for bit in range(1, batch_bits)]
    steps = [(("b", 0), ("b", 0))] if batch_bits else []
    steps += list(zip(middle, reversed(middle)))
    return steps + [(("z", bit), ("z", bit)) for bit in range(blk_bits)]


def step_partner(step):
    def partner(b, z):
        axis, bit = step[b & 1]
        return (b ^ (1 << bit), z) if axis == "b" else (b, z ^ (1 << bit))

    return partner


def own_bit(step):
    b, z = lax.axis_index("batch"), lax.axis_index("blk")

    def value(part):
        return ((b if part[0] == "b" else z) >> part[1]) & 1

    return jnp.where(b & 1 == 1, value(step[1]), value(step[0])).astype(jnp.int32)


def add_halves(keep, got, bit):
    def half(which):
        shape = (2, keep.shape[0] // 2) + keep.shape[1:]
        mine = lax.dynamic_index_in_dim(keep.reshape(shape), which, 0, False)
        other = lax.dynamic_index_in_dim(got.reshape(shape), which, 0, False)
        return (mine.astype(f32) + other.astype(f32)).astype(bf16)

    return half(1 - bit), half(bit)


def sum_matrix(send, keep, sizes):
    steps = halving_steps(sizes)
    bits = [own_bit(step) for step in steps]
    for i, step in enumerate(steps):
        got = move(send, sizes, step_partner(step))
        if i + 1 < len(steps):
            send, keep = add_halves(keep, got, bits[i + 1])
        else:
            keep = (keep.astype(f32) + got.astype(f32)).astype(bf16)
    for i in reversed(range(len(steps))):
        got = move(keep, sizes, step_partner(steps[i]))
        if i > 0:
            bit = bits[i]
            keep = jnp.concatenate(
                [jnp.where(bit == 0, keep, got), jnp.where(bit == 0, got, keep)], axis=0
            )
        else:
            keep = join(keep, got, bits[i].reshape(1), f32, keep.shape[0] // 2)
    return keep


def sum_small(array, sizes):
    for step in halving_steps(sizes):
        array = array + move(array, sizes, step_partner(step))
    return array


def per_device(
    hidden_in,
    lengths,
    qkv_weight,
    qv_bias,
    out_weight,
    out_bias,
    attn_gain,
    attn_shift,
    up_weight,
    up_bias,
    down_weight,
    down_bias,
    ffn_gain,
    ffn_shift,
    head_weight,
    head_bias,
    hidden_cot,
    term_cot,
):
    row_count, seg_len, d = hidden_in.shape
    hidden = up_weight.shape[1]
    parts = hidden // d
    sizes = (lax.axis_size("batch"), lax.axis_size("blk"))
    nz = sizes[1]
    own_rows = row_count // nz
    n = seg_len * nz
    tile = n // 2
    rows = range(own_rows)
    core = (lax.axis_index("batch") & 1).astype(jnp.int32).reshape(1)

    x = [jnp.concatenate(to_rows(hidden_in, sizes, r), axis=0) for r in rows]
    cot = [jnp.concatenate(to_rows(hidden_cot, sizes, r), axis=0) for r in rows]
    own_slots = lax.all_gather(term_cot, "blk", axis=0)
    own_slots = jnp.stack([
        lax.dynamic_index_in_dim(own_slots, (lax.axis_index("blk") - k) % nz, 0, False)
        for k in range(nz)
    ], axis=1)
    own_slots = lax.dynamic_slice_in_dim(
        own_slots, lax.axis_index("blk") * own_rows, own_rows, 0
    ).reshape(own_rows, 1, n)

    vec = jnp.concatenate(
        [
            qv_bias,
            out_bias[None],
            attn_gain[None],
            attn_shift[None],
            down_bias[None],
            ffn_gain[None],
            ffn_shift[None],
            head_weight[None],
            jnp.broadcast_to(head_bias[None], (1, d)),
            up_bias.reshape(parts, d),
            jnp.zeros((-(V_UP + parts) % 8, d), bf16),
        ],
        axis=0,
    ).astype(f32)

    att, back = [], []
    for r in rows:
        q, k, v, a, probs = attend(x[r], lengths, qkv_weight, vec, nz, own_rows, r)
        att.append(a)
        back.append((q, k, v, a, probs))
    fed = [feed(x[r], att[r], out_weight, up_weight, down_weight, vec, tile) for r in rows]
    hid, term, act, slope, low, n1, n2, stats = zip(*fed)
    hidden_out = to_segments(
        [[hid[r][k * seg_len : (k + 1) * seg_len] for k in range(nz)] for r in rows], sizes
    )
    term_weight = to_segments(
        [[term[r][0, k * seg_len : (k + 1) * seg_len] for k in range(nz)] for r in rows], sizes
    )
    fg, head_sums = zip(
        *[head_back(cot[r], own_slots[r], n2[r], stats[r], vec, tile) for r in rows]
    )
    down = [weight_grad(act, fg, w, 384) for w in (1 - core, core)]
    gate_grad, ag, feed_sums = zip(
        *[feed_back(fg[r], slope[r], n1[r], stats[r], up_weight, down_weight, vec, tile) for r in rows]
    )
    up = [weight_grad(low, [g[None] for g in gate_grad], w, 768) for w in (1 - core, core)]
    out = [weight_grad(att, ag, w, 384) for w in (1 - core, core)]
    backs = [attend_back(ag[r], out_weight, *back[r], qkv_weight) for r in rows]
    proj_grad, gh, qv_sums = zip(*backs)
    qkv = [weight_grad(x, proj_grad, w, 768) for w in (1 - core, core)]
    grad_hidden = to_segments(
        [[gh[r][k * seg_len : (k + 1) * seg_len] for k in range(nz)] for r in rows], sizes
    ).astype(f32)

    early = sum_small(jnp.concatenate([sum(head_sums), sum(feed_sums)], axis=0), sizes)
    late = sum_small(sum(qv_sums), sizes)
    grad_down, grad_up, grad_out, grad_qkv = [
        sum_matrix(*pair, sizes) for pair in (down, up, out, qkv)
    ]
    return (
        hidden_out,
        term_weight,
        grad_hidden,
        grad_qkv,
        late[0:2],
        grad_out,
        early[10],
        early[8],
        early[9],
        grad_up,
        early[11 : 11 + parts].reshape(hidden),
        grad_down,
        early[3],
        early[0],
        early[1],
        early[2],
        early[4, 0:1],
    )


def solution(mesh):
    split = P("batch", "blk", None)
    flat = P("batch", "blk")
    return jax.shard_map(
        per_device,
        mesh=mesh,
        in_specs=(split, P("batch", None)) + (P(),) * 14 + (split, flat),
        out_specs=(split, flat, split) + (P(),) * 14,
        check_vma=False,
    )
```

```python
import functools

import jax
import jax.numpy as jnp
from jax import lax
from jax.experimental import pallas as pl
from jax.experimental.pallas import tpu as pltpu
from jax.sharding import PartitionSpec as P

HD = 64
PACK = 16
AXES = ("batch", "blk")
epsilon = 1e-06
masked_score = -1e30
f32 = jnp.float32
bf16 = jnp.bfloat16
NT = (((1,), (1,)), ((), ()))
TN = (((0,), (0,)), ((), ()))

(
    V_QUERY,
    V_VALUE,
    V_OUT,
    V_GAIN1,
    V_SHIFT1,
    V_DOWN,
    V_GAIN2,
    V_SHIFT2,
    V_HEAD,
    V_HEAD_BIAS,
    V_UP,
) = range(11)


def dot(left, right, dims=None):
    if dims is None:
        return jnp.dot(left, right, preferred_element_type=f32)
    return lax.dot_general(left, right, dims, preferred_element_type=f32)


def call_params(mebibytes):
    return pltpu.CompilerParams(vmem_limit_bytes=mebibytes * 2**20)


TIMES = {
    "attend": 11,
    "feed": 20,
    "feed_back": 18,
    "head_back": 2,
    "attend_back": 13,
    "weight_rows": 5,
    "weight_up": 5,
    "weight_qkv": 3,
}


class Order:
    def __init__(self):
        self.token = None

    def run(self, kernel, args, in_specs, out_specs, out_shape, grid, memory, name, **extra):
        prefetch = extra.pop("prefetch", 0)
        scratch = extra.pop("scratch", ())
        single = not isinstance(out_shape, list)
        if single:
            out_specs, out_shape = [out_specs], [out_shape]
        count, made = len(args), len(out_shape)
        tokens = [] if self.token is None else [self.token]

        def body(*refs):
            outs = refs[count + len(tokens) :]
            outs[made][...] = jnp.zeros((8, 128), f32)
            kernel(*refs[:count], *outs[:made], *outs[made + 1 :])

        results = pl.pallas_call(
            body,
            grid_spec=pltpu.PrefetchScalarGridSpec(
                num_scalar_prefetch=prefetch,
                grid=grid,
                in_specs=list(in_specs) + [pl.BlockSpec(memory_space=pl.ANY)] * len(tokens),
                out_specs=list(out_specs) + [pl.BlockSpec((8, 128), lambda *i: (0, 0))],
                scratch_shapes=list(scratch),
            ),
            out_shape=list(out_shape) + [jax.ShapeDtypeStruct((8, 128), f32)],
            compiler_params=call_params(memory),
            cost_estimate=pl.CostEstimate(
                flops=int(TIMES.get(name, 1) * 1e10), bytes_accessed=1000, transcendentals=0
            ),
            name=name,
            **extra,
        )(*args, *tokens)
        self.token = results[-1]
        return results[0] if single else results[:-1]


def whole(array, buffers=None):
    spec = {} if buffers is None else {"pipeline_mode": pl.Buffered(buffers)}
    return pl.BlockSpec(array.shape, lambda *i: (0,) * array.ndim, **spec)


def in_vmem():
    return pl.BlockSpec(memory_space=pltpu.VMEM)


def in_hbm(array):
    return pltpu.with_memory_space_constraint(array, pltpu.HBM)


def column_sum(values):
    return jnp.sum(values, axis=0, keepdims=True)


def row_mean(values):
    return jnp.mean(values, axis=-1, keepdims=True)


def to_column(row, count):
    return jnp.transpose(jnp.broadcast_to(row, (128, count)))[:, 0:1]


def to_row(column, count):
    return jnp.transpose(jnp.broadcast_to(column, (count, 128)))[0:1, :]


def attend_kernel(nz, own_rows, row, lengths, *refs):
    blocks = refs[:nz]
    wq, wk, wv, vec = refs[nz : nz + 4]
    x_ref, q_ref, k_ref, v_ref, att_ref, p_ref, bias = refs[-7:]
    seg_len = blocks[0].shape[0]
    step = pl.program_id(0)
    width = q_ref.shape[1]

    @pl.when(step == 0)
    def _():
        z = lax.axis_index("blk")
        mine = z * own_rows + row
        cols, rows = [], []
        for k in range(nz):
            x_ref[pl.ds(k * seg_len, seg_len), :] = blocks[k][...]
            base = lax.rem(z + (nz - k), nz) * seg_len
            col = lax.broadcasted_iota(jnp.int32, (seg_len, 1), 0) + base
            lane = lax.broadcasted_iota(jnp.int32, (1, seg_len), 1) + base
            end = jnp.int32(0)
            doc_col, doc_row = jnp.zeros_like(col), jnp.zeros_like(lane)
            for p in range(lengths.shape[1]):
                end = end + lengths[mine, p]
                doc_col += (col >= end).astype(jnp.int32)
                doc_row += (lane >= end).astype(jnp.int32)
            cols.append(doc_col)
            rows.append(doc_row)
        for i in range(nz):
            for j in range(nz):
                bias[pl.ds(i * seg_len, seg_len), pl.ds(j * seg_len, seg_len)] = jnp.where(
                    cols[i] == rows[j], 0.0, masked_score
                ).astype(f32)

    x = x_ref[...]
    q_ref[...] = (dot(x, wq[...]) + vec[V_QUERY : V_QUERY + 1, :]).astype(bf16)
    k_ref[...] = dot(x, wk[...]).astype(bf16)
    v_ref[...] = (dot(x, wv[...]) + vec[V_VALUE : V_VALUE + 1, :]).astype(bf16)
    first = lax.broadcasted_iota(jnp.int32, (1, 2 * HD), 1) < HD
    for pair in range(width // (2 * HD)):
        cols = pl.ds(pair * 2 * HD, 2 * HD)
        q, k, v = q_ref[:, cols], k_ref[:, cols], v_ref[:, cols]
        outs = []
        for h in range(2):
            mine = first if h == 0 else jnp.logical_not(first)
            scaled = jnp.where(mine, q * jnp.asarray(HD**-0.5, bf16), jnp.zeros_like(q))
            scores = dot(scaled, k, NT) + bias[...]
            weights = jnp.exp(scores - jnp.max(scores, axis=1, keepdims=True))
            total = jnp.sum(weights, axis=1, keepdims=True)
            probs = (weights * (1.0 / total)).astype(bf16)
            p_ref[pair * 2 + h] = probs
            outs.append(dot(probs, v))
        att_ref[:, cols] = jnp.where(first, outs[0], outs[1]).astype(bf16)


def weight_columns(d, width, steps, part):
    return pl.BlockSpec((d, width), lambda j: (0, part * steps + j))


def attend(order, blocks, lengths, wqkv, vec, own_rows, row, before, width=256):
    seg_len, d = blocks[0].shape
    nz = len(blocks)
    n = nz * seg_len
    steps, heads = d // width, width // HD
    token = pl.BlockSpec((n, width), lambda j: (row, j))
    first = 1 + nz + 4
    return order.run(
        functools.partial(attend_kernel, nz, own_rows, row),
        [lengths, *blocks, *[in_hbm(wqkv)] * 3, vec, *before],
        [pl.BlockSpec(memory_space=pltpu.SMEM)]
        + [whole(b, 1) for b in blocks]
        + [weight_columns(d, width, steps, part) for part in range(3)]
        + [pl.BlockSpec((vec.shape[0], width), lambda j: (0, j))]
        + [pl.BlockSpec(memory_space=pl.ANY)] * len(before),
        [pl.BlockSpec((n, d), lambda j: (row, 0))]
        + [token] * 4
        + [pl.BlockSpec((heads, n, n), lambda j: (row * steps + j, 0, 0))],
        [jax.ShapeDtypeStruct((own_rows * n, d), bf16)] * 5
        + [pltpu.HBM((own_rows * d // HD, n, n), bf16)],
        (steps,),
        18,
        "attend",
        scratch=[pltpu.VMEM((n, n), f32)],
        input_output_aliases={first + i: i for i in range(len(before))},
    )


def attend_back_kernel(nz, steps, g_ref, wo, q_ref, k_ref, v_ref, att_ref, p_ref, wq, wk, wv, *refs):
    dp_ref, sums, acc, up_s = refs[-nz - 4 : -nz - 2] + refs[-2:]
    gh_refs = refs[-nz - 2 : -2]
    step = pl.program_id(0)
    width = q_ref.shape[1]

    def part(i):
        return pl.ds(pl.multiple_of((i * steps + step) * width, width), width)

    up_s[...] = dot(g_ref[...], wo[...], NT).astype(bf16)
    first = lax.broadcasted_iota(jnp.int32, (1, 2 * HD), 1) < HD
    scale = HD**-0.5
    grads = [[], [], []]
    for pair in range(width // (2 * HD)):
        cols = pl.ds(pair * 2 * HD, 2 * HD)
        q, k, v, up = q_ref[:, cols], k_ref[:, cols], v_ref[:, cols], up_s[:, cols]
        product = up.astype(f32) * att_ref[:, cols].astype(f32)
        dq, dk, dv = [], [], []
        for h in range(2):
            mine = first if h == 0 else jnp.logical_not(first)
            inner = jnp.sum(jnp.where(mine, product, 0.0), axis=1, keepdims=True)
            probs = p_ref[pair * 2 + h]
            dprobs = dot(jnp.where(mine, up, jnp.zeros_like(up)), v, NT)
            score_grad = (probs.astype(f32) * (dprobs - inner)).astype(bf16)
            dv.append(dot(probs, up, TN))
            dq.append(dot(score_grad, k))
            dk.append(dot(score_grad, q, TN))
        grads[0].append((jnp.where(first, dq[0], dq[1]) * scale).astype(bf16))
        grads[1].append((jnp.where(first, dk[0], dk[1]) * scale).astype(bf16))
        grads[2].append(jnp.where(first, dv[0], dv[1]).astype(bf16))
    grads = [jnp.concatenate(g, axis=1) for g in grads]
    total = 0
    for i, weight in enumerate((wq, wk, wv)):
        dp_ref[:, part(i)] = grads[i]
        total += dot(grads[i], weight[...], NT)
    sums[...] = jnp.zeros_like(sums)
    sums[0:1, :] = column_sum(grads[0].astype(f32))
    sums[1:2, :] = column_sum(grads[2].astype(f32))

    @pl.when(step == 0)
    def _():
        acc[...] = g_ref[...].astype(f32) + total

    @pl.when(step > 0)
    def _():
        acc[...] += total

    @pl.when(step == pl.num_programs(0) - 1)
    def _():
        seg_len = acc.shape[0] // nz
        for k in range(nz):
            gh_refs[k][0] = acc[pl.ds(k * seg_len, seg_len), :].astype(bf16)


def attend_back(order, g, wo, q, k, v, att, probs, wqkv, nz, own_rows, row, before, width=256):
    d = g.shape[1]
    n = g.shape[0] // own_rows
    steps, heads = d // width, width // HD
    seg_len = n // nz
    token = pl.BlockSpec((n, width), lambda j: (row, j))
    return order.run(
        functools.partial(attend_back_kernel, nz, steps),
        [g, wo, q, k, v, att, in_hbm(probs), *[in_hbm(wqkv)] * 3, *before],
        [
            pl.BlockSpec((n, d), lambda j: (row, 0), pipeline_mode=pl.Buffered(1)),
            pl.BlockSpec((width, d), lambda j: (j, 0)),
            token,
            token,
            token,
            token,
            pl.BlockSpec((heads, n, n), lambda j: (row * steps + j, 0, 0)),
        ]
        + [weight_columns(d, width, steps, i) for i in range(3)]
        + [pl.BlockSpec(memory_space=pl.ANY)] * len(before),
        [
            pl.BlockSpec((n, 3 * d), lambda j: (row, 0)),
            pl.BlockSpec((8, width), lambda j: (row, j)),
        ]
        + [pl.BlockSpec((1, seg_len, d), lambda j: (0, 0, 0))] * nz,
        [
            jax.ShapeDtypeStruct((own_rows * n, 3 * d), bf16),
            jax.ShapeDtypeStruct((own_rows * 8, d), f32),
        ]
        + [jax.ShapeDtypeStruct((1, seg_len, d), bf16)] * nz,
        (steps,),
        22,
        "attend_back",
        scratch=[pltpu.VMEM((n, d), f32), pltpu.VMEM((n, width), bf16)],
        input_output_aliases={10 + i: i for i in range(len(before))},
    )


def split_term(row):
    high = row.astype(bf16)
    rest = (row - high.astype(f32)).astype(bf16)
    return jnp.concatenate([high, rest, jnp.zeros((PACK - 2, row.shape[1]), bf16)], axis=0)


def join_term(rows):
    return rows[0:1].astype(f32) + rows[1:2].astype(f32)


def feed_kernel(nz, seg_len, x_ref, att_ref, wo, wu, wd, vec, *refs):
    act, slope, low, n1_ref, n2_ref, stats = refs[-nz - 6 : -nz]
    hid = refs[-nz:]
    n, d = x_ref.shape
    parts = act.shape[1] // d

    def row(i):
        return vec[i : i + 1, :]

    first_sum = x_ref[...].astype(f32) + dot(att_ref[...], wo[...]) + row(V_OUT)
    center = first_sum - row_mean(first_sum)
    scale1 = lax.rsqrt(row_mean(center * center) + epsilon)
    n1 = center * scale1
    n1_ref[...] = n1.astype(bf16)
    normed = n1 * row(V_GAIN1) + row(V_SHIFT1)
    normed_low = normed.astype(bf16)
    low[...] = normed_low
    second_sum = normed + row(V_DOWN)
    for c in range(parts):
        cols = pl.ds(c * d, d)
        gate = dot(normed_low, wu[:, cols]) + row(V_UP + c)
        below = 0.5 * (1.0 + lax.erf(gate * (0.5**0.5)))
        density = jnp.exp(-0.5 * gate * gate) * 0.3989422804014327
        active = (gate * below).astype(bf16)
        act[:, cols] = active
        slope[:, cols] = (below + gate * density).astype(bf16)
        second_sum += dot(active, wd[cols, :])
    center = second_sum - row_mean(second_sum)
    scale2 = lax.rsqrt(row_mean(center * center) + epsilon)
    n2 = center * scale2
    n2_ref[...] = n2.astype(bf16)
    final = n2 * row(V_GAIN2) + row(V_SHIFT2)
    logits = jnp.sum(final * row(V_HEAD), axis=1, keepdims=True) + vec[V_HEAD_BIAS, 0]
    term = jnp.maximum(logits, 0.0) + jnp.log1p(jnp.exp(-jnp.abs(logits)))
    count = n // seg_len
    for k in range(nz):

        @pl.when(lax.rem(pl.program_id(0), nz // count) == k // count)
        def _():
            rows = slice((k % count) * seg_len, (k % count + 1) * seg_len)
            hid[k][0, 0:seg_len, :] = final[rows].astype(bf16)
            hid[k][0, seg_len:, 0:seg_len] = split_term(to_row(term[rows], seg_len))

    lane = lax.broadcasted_iota(jnp.int32, (1, 128), 1)
    stats[...] = jnp.where(lane == 0, scale1, jnp.where(lane == 1, scale2, logits))


def feed(order, x, att, wo, wu, wd, vec, nz, own_rows):
    d = x.shape[1]
    n = x.shape[0] // own_rows
    seg_len = n // nz
    tile = seg_len * max(1, nz // 2)
    per_row = n // tile
    hidden = wu.shape[1]
    token = pl.BlockSpec((tile, d), lambda i: (i, 0))
    wide = pl.BlockSpec((tile, hidden), lambda i: (i, 0))
    total = own_rows * n
    return order.run(
        functools.partial(feed_kernel, nz, seg_len),
        [x, att, wo, wu, wd, vec],
        [token, token, in_vmem(), in_vmem(), in_vmem(), whole(vec, 1)],
        [wide, wide, token, token, token, pl.BlockSpec((tile, 128), lambda i: (i, 0))]
        + [pl.BlockSpec((1, seg_len + PACK, d), lambda i: (i // per_row, 0, 0))] * nz,
        [
            pltpu.HBM((total, hidden), bf16),
            pltpu.HBM((total, hidden), bf16),
            jax.ShapeDtypeStruct((total, d), bf16),
            jax.ShapeDtypeStruct((total, d), bf16),
            jax.ShapeDtypeStruct((total, d), bf16),
            jax.ShapeDtypeStruct((total, 128), f32),
        ]
        + [jax.ShapeDtypeStruct((own_rows, seg_len + PACK, d), bf16)] * nz,
        (total // tile,),
        22,
        "feed",
    )


def head_back_kernel(nz, n2_ref, stats, vec, *refs):
    cots, fg, sums = refs[:nz], refs[nz], refs[nz + 1]
    d = fg.shape[1]
    seg_len = fg.shape[0] // nz

    def row(i):
        return vec[i : i + 1, :]

    total = jnp.zeros(sums.shape, f32)
    for k in range(nz):
        tokens = pl.ds(k * seg_len, seg_len)
        n2 = n2_ref[tokens, :].astype(f32)
        scale2, logits = stats[tokens, 1:2], stats[tokens, 2:3]
        term_cot = to_column(join_term(cots[k][0, seg_len:, 0:seg_len]), seg_len)
        term_grad = term_cot * (1.0 / (1.0 + jnp.exp(-logits)))
        final_grad = cots[k][0, 0:seg_len, :].astype(f32) + term_grad * row(V_HEAD)
        gained = final_grad * row(V_GAIN2)
        grad = (gained - row_mean(gained) - n2 * row_mean(gained * n2)) * scale2
        grad_low = grad.astype(bf16)
        fg[tokens, :] = grad_low
        total += jnp.concatenate(
            [
                column_sum(final_grad * n2),
                column_sum(final_grad),
                column_sum(term_grad * (n2 * row(V_GAIN2) + row(V_SHIFT2))),
                column_sum(grad_low.astype(f32)),
                jnp.broadcast_to(column_sum(term_grad), (1, d)),
                jnp.zeros((3, d), f32),
            ],
            axis=0,
        )
    @pl.when(pl.program_id(0) == 0)
    def _():
        sums[...] = total

    @pl.when(pl.program_id(0) > 0)
    def _():
        sums[...] += total


def head_back(order, cots, n2, stats, vec):
    own_rows, _, d = cots[0].shape
    n = n2.shape[0] // own_rows
    nz = len(cots)
    token = pl.BlockSpec((n, d), lambda i: (i, 0))
    return order.run(
        functools.partial(head_back_kernel, nz),
        [n2, stats, vec, *cots],
        [token, pl.BlockSpec((n, 128), lambda i: (i, 0)), whole(vec, 1)]
        + [pl.BlockSpec((1,) + cots[0].shape[1:], lambda i: (i, 0, 0))] * nz,
        [token, pl.BlockSpec((8, d), lambda i: (0, 0))],
        [jax.ShapeDtypeStruct(n2.shape, bf16), jax.ShapeDtypeStruct((8, d), f32)],
        (own_rows,),
        12,
        "head_back",
    )


def feed_back_kernel(fg_ref, slope, n1_ref, stats, wu, wd, vec, gate_grad, ag, sums):
    d = fg_ref.shape[1]
    parts = slope.shape[1] // d
    fg = fg_ref[...]
    total = fg.astype(f32)
    ups = []
    for c in range(parts):
        cols = pl.ds(c * d, d)
        grad = (dot(fg, wd[cols, :], NT) * slope[:, cols].astype(f32)).astype(bf16)
        gate_grad[:, cols] = grad
        ups.append(column_sum(grad.astype(f32)))
        total += dot(grad, wu[:, cols], NT)
    n1 = n1_ref[...].astype(f32)
    gained = total * vec[V_GAIN1 : V_GAIN1 + 1, :]
    low = ((gained - row_mean(gained) - n1 * row_mean(gained * n1)) * stats[:, 0:1]).astype(bf16)
    ag[...] = low
    part = jnp.concatenate(
        [column_sum(total * n1), column_sum(total), column_sum(low.astype(f32))]
        + ups
        + [jnp.zeros((sums.shape[0] - 3 - parts, d), f32)],
        axis=0,
    )

    @pl.when(pl.program_id(0) == 0)
    def _():
        sums[...] = part

    @pl.when(pl.program_id(0) > 0)
    def _():
        sums[...] += part


def feed_back(order, fg, slope, n1, stats, wu, wd, vec, tile):
    n, d = fg.shape
    hidden = wu.shape[1]
    count = -(-(3 + hidden // d) // 8) * 8
    token = pl.BlockSpec((tile, d), lambda i: (i, 0))
    wide = pl.BlockSpec((tile, hidden), lambda i: (i, 0))
    return order.run(
        feed_back_kernel,
        [fg, in_hbm(slope), n1, stats, wu, wd, vec],
        [
            token,
            wide,
            token,
            pl.BlockSpec((tile, 128), lambda i: (i, 0)),
            in_vmem(),
            in_vmem(),
            whole(vec, 1),
        ],
        [wide, token, pl.BlockSpec((count, d), lambda i: (0, 0))],
        [pltpu.HBM((n, hidden), bf16), jax.ShapeDtypeStruct((n, d), bf16), jax.ShapeDtypeStruct((count, d), f32)],
        (n // tile,),
        20,
        "feed_back",
    )


def weight_rows_kernel(which, left, right, out):
    out[...] = dot(left[...], right[...], TN).astype(bf16)


def weight_rows(order, left, right, which, block):
    n, rows = left.shape
    half, width = rows // 2, right.shape[1]
    return order.run(
        weight_rows_kernel,
        [which, in_hbm(left), right],
        [
            pl.BlockSpec((n, block), lambda j, w: (0, w[0] * (half // block) + j)),
            whole(right, 1),
        ],
        pl.BlockSpec((block, width), lambda j, w: (j, 0)),
        jax.ShapeDtypeStruct((half, width), bf16),
        (half // block,),
        12,
        "weight_rows",
        prefetch=1,
    )


def weight_up_kernel(which, low, att, gate, ag, out):
    chunk = which[0] * 2 + pl.program_id(0)

    @pl.when(chunk < 3)
    def _():
        out[...] = dot(low[...], gate[...], TN).astype(bf16)

    @pl.when(chunk == 3)
    def _():
        width = ag.shape[1]
        out[:, 0:width] = dot(att[...], ag[...], TN).astype(bf16)
        out[:, width:] = jnp.zeros((out.shape[0], out.shape[1] - width), bf16)


def weight_up(order, low, att, gate, ag, which):
    n, d = low.shape
    width = gate.shape[1] // 3
    return order.run(
        weight_up_kernel,
        [which, low, att, in_hbm(gate), ag],
        [
            whole(low, 1),
            whole(att, 1),
            pl.BlockSpec((n, width), lambda j, w: (0, jnp.minimum(w[0] * 2 + j, 2))),
            whole(ag, 1),
        ],
        pl.BlockSpec((d, width), lambda j, w: (j, 0)),
        jax.ShapeDtypeStruct((2 * d, width), bf16),
        (2,),
        18,
        "weight_up",
        prefetch=1,
    )


def weight_qkv_kernel(which, x, grad, out):
    width = out.shape[1]
    chunk = which[0] * 2 + pl.program_id(0)

    @pl.when(chunk < 3)
    def _():
        cols = pl.ds(pl.multiple_of(chunk * width, 128), width)
        out[...] = dot(x[...], grad[:, cols], TN).astype(bf16)

    @pl.when(chunk == 3)
    def _():
        last = grad.shape[1] - 3 * width
        out[:, 0:last] = dot(x[...], grad[:, 3 * width :], TN).astype(bf16)
        out[:, last:] = jnp.zeros((out.shape[0], width - last), bf16)


def weight_qkv(order, x, grad, which):
    d = x.shape[1]
    width = (grad.shape[1] + 256) // 4
    return order.run(
        weight_qkv_kernel,
        [which, x, grad],
        [whole(x, 1), whole(grad, 1)],
        pl.BlockSpec((d, width), lambda j, w: (j, 0)),
        jax.ShapeDtypeStruct((2 * d, width), bf16),
        (2,),
        16,
        "weight_qkv",
        prefetch=1,
    )


def add_kernel(bit, keep_a, got_a, keep_b, got_b, send, keep):
    send[...] = (keep_a[...].astype(f32) + got_a[...].astype(f32)).astype(bf16)
    keep[...] = (keep_b[...].astype(f32) + got_b[...].astype(f32)).astype(bf16)


def add_halves(order, keep, got, bit):
    rows, width = keep.shape
    half = rows // 2
    if half % 16:
        total = (keep.astype(f32) + got.astype(f32)).astype(bf16).reshape(2, half, width)
        return (
            lax.dynamic_index_in_dim(total, 1 - bit[0], 0, False),
            lax.dynamic_index_in_dim(total, bit[0], 0, False),
        )
    steps = 2 if half * width > 400_000 else 1
    block = half // steps
    away = pl.BlockSpec((block, width), lambda i, b: ((1 - b[0]) * steps + i, 0))
    stay = pl.BlockSpec((block, width), lambda i, b: (b[0] * steps + i, 0))
    out = pl.BlockSpec((block, width), lambda i, b: (i, 0))
    return order.run(
        add_kernel,
        [bit, keep, got, keep, got],
        [away, away, stay, stay],
        [out, out],
        [jax.ShapeDtypeStruct((half, width), bf16)] * 2,
        (steps,),
        12,
        "add_halves",
        prefetch=1,
    )


def add_last_kernel(keep, got, out):
    out[...] = (keep[...].astype(f32) + got[...].astype(f32)).astype(bf16)


def add_last(order, keep, got):
    if keep.shape[0] % 16:
        return (keep.astype(f32) + got.astype(f32)).astype(bf16)
    return order.run(
        add_last_kernel,
        [keep, got],
        [whole(keep, 1), whole(got, 1)],
        pl.BlockSpec(keep.shape, lambda i: (0, 0)),
        jax.ShapeDtypeStruct(keep.shape, bf16),
        (1,),
        8,
        "add_last",
    )


def pair_kernel(bit, mine, other, out):
    rows = mine.shape[0]
    out[pl.ds(pl.multiple_of(bit[0] * rows, 16), rows), :] = mine[...]
    out[pl.ds(pl.multiple_of((1 - bit[0]) * rows, 16), rows), :] = other[...]


def pair(order, mine, other, bit):
    rows, width = mine.shape
    if rows % 16:
        first = bit[0] == 0
        return jnp.concatenate([jnp.where(first, mine, other), jnp.where(first, other, mine)])
    return order.run(
        pair_kernel,
        [bit, mine, other],
        [pl.BlockSpec((rows, width), lambda i, b: (0, 0))] * 2,
        pl.BlockSpec((2 * rows, width), lambda i, b: (0, 0)),
        jax.ShapeDtypeStruct((2 * rows, width), bf16),
        (1,),
        8,
        "pair",
        prefetch=1,
    )


def join_kernel(where, *refs):
    for i in range(4):

        @pl.when(pl.program_id(0) == where[i])
        def _():
            refs[4][...] = refs[i][...].astype(f32)


def join_rows(order, pieces, where, block=384):
    rows, width = pieces[0].shape
    steps = rows // block
    return order.run(
        join_kernel,
        [where, *pieces],
        [piece_spec(i, block, width, steps) for i in range(4)],
        pl.BlockSpec((block, width), lambda c, j, w: (c * steps + j, 0)),
        pltpu.HBM((4 * rows, width), f32),
        (4, steps),
        12,
        "join_rows",
        prefetch=1,
    )


def piece_spec(i, block, width, steps):
    def place(c, j, w):
        return (jnp.where(c == w[i], j, jnp.where(c < w[i], 0, steps - 1)), 0)

    return pl.BlockSpec((block, width), place)


def join_columns_kernel(whole_chunks, left, extra, where, *refs):
    pieces, outs = refs[:4], refs[4:]
    chunk = pl.program_id(0)
    for i in range(4):

        @pl.when(jnp.logical_and(chunk == where[i], chunk < whole_chunks))
        def _():
            outs[0][...] = pieces[i][...].astype(f32)

        @pl.when(jnp.logical_and(chunk == where[i], chunk >= whole_chunks))
        def _():
            if left:
                outs[0][:, 0:left] = pieces[i][:, 0:left].astype(f32)
            if extra:
                outs[1][...] = pieces[i][:, left : left + extra].astype(f32)


def join_columns(order, pieces, where, width_out, extra=0, block=384):
    rows, width = pieces[0].shape
    steps = rows // block
    whole_chunks = width_out // width
    left = width_out - whole_chunks * width
    end = whole_chunks if left else whole_chunks - 1

    def place(c, j, w):
        return (jnp.where(c > end, steps - 1, j), jnp.minimum(c, end))

    def at_last(c, j):
        return jnp.where(c == 3, j, 0)

    out_specs = [pl.BlockSpec((block, width), place)]
    out_shape = [pltpu.HBM((rows, width_out), f32)]
    if extra:
        out_specs.append(pl.BlockSpec((block, extra), lambda c, j, w: (at_last(c, j), 0)))
        out_shape.append(pltpu.HBM((rows, extra), f32))
    return order.run(
        functools.partial(join_columns_kernel, whole_chunks, left, extra),
        [where, *pieces],
        [piece_spec(i, block, width, steps) for i in range(4)],
        out_specs,
        out_shape,
        (4, steps),
        14,
        "join_columns",
        prefetch=1,
    )


def hold_kernel(array, out):
    pass


def hold(order, array):
    return order.run(
        hold_kernel,
        [array],
        [pl.BlockSpec(memory_space=pl.ANY)],
        pl.BlockSpec(memory_space=pl.ANY),
        jax.ShapeDtypeStruct(array.shape, array.dtype),
        (1,),
        4,
        "hold",
        input_output_aliases={0: 0},
    )


def pick_kernel(order, *refs):
    k = pl.program_id(0)
    for i, out in enumerate(refs[1:]):

        @pl.when(k == i)
        def _():
            out[...] = refs[0][...]


def pick(order, local, places, first, count):
    nz = places.shape[0]
    own_rows = local.shape[0] // nz
    shape = (count,) + local.shape[1:]
    return order.run(
        pick_kernel,
        [places, local],
        [pl.BlockSpec(shape, lambda k, o: ((o[k] * own_rows + first) // count, 0, 0))],
        [pl.BlockSpec(shape, lambda k, o: (0, 0, 0))] * nz,
        [jax.ShapeDtypeStruct(shape, local.dtype)] * nz,
        (nz,),
        8,
        "pick",
        prefetch=1,
    )


def place_kernel(nz, order, *refs):
    outs = refs[-2:] if len(refs[-1].shape) == 3 else refs[-1:]
    seg_len = outs[0].shape[2]
    for i in range(nz):

        @pl.when(pl.program_id(0) == i)
        def _():
            block = refs[i]
            outs[0][0] = block[:, 0:seg_len, :].astype(outs[0].dtype)
            if len(outs) > 1:
                for r in range(block.shape[0]):
                    outs[1][0, r : r + 1, :] = join_term(block[r, seg_len:, 0:seg_len])


def place(order, blocks, places, own_rows, seg_len, dtype, row=0, before=(), with_term=False):
    nz = len(blocks)
    count, _, d = blocks[0].shape
    out_shape = [pltpu.HBM((nz, own_rows, seg_len, d), dtype)]
    out_specs = [pl.BlockSpec((1, count, seg_len, d), lambda k, o: (o[k], row, 0, 0))]
    if with_term:
        out_shape.append(jax.ShapeDtypeStruct((nz, own_rows, seg_len), f32))
        out_specs.append(pl.BlockSpec((1, count, seg_len), lambda k, o: (o[k], row, 0)))
    return order.run(
        functools.partial(place_kernel, nz),
        [places, *blocks, *before],
        [whole(b, 1) for b in blocks] + [pl.BlockSpec(memory_space=pl.ANY)] * len(before),
        out_specs,
        out_shape,
        (nz,),
        10,
        "place",
        prefetch=1,
        input_output_aliases={1 + nz + i: i for i in range(len(before))},
    )


def bits_of(count):
    return max(count - 1, 0).bit_length()


def move(array, sizes, partner):
    pairs = []
    for b in range(sizes[0]):
        for z in range(sizes[1]):
            to_b, to_z = partner(b, z)
            pairs.append((b * sizes[1] + z, to_b * sizes[1] + to_z))
    return lax.ppermute(array, AXES, pairs)


def send_round(blocks, sizes, sign):
    nz = sizes[1]
    return [blocks[0]] + [
        move(blocks[k], sizes, lambda b, z, k=k: (b, (z + sign * k) % nz)) for k in range(1, nz)
    ]


def halving_steps(sizes):
    batch_bits, blk_bits = bits_of(sizes[0]), bits_of(sizes[1])
    middle = [("b", bit) for bit in range(1, batch_bits)]
    steps = [(("b", 0), ("b", 0))] if batch_bits else []
    steps += list(zip(middle, reversed(middle)))
    return steps + [(("z", bit), ("z", bit)) for bit in range(blk_bits)]


def step_partner(step):
    def partner(b, z):
        axis, bit = step[b & 1]
        return (b ^ (1 << bit), z) if axis == "b" else (b, z ^ (1 << bit))

    return partner


def own_bit(step):
    b, z = lax.axis_index("batch"), lax.axis_index("blk")

    def value(part):
        return ((b if part[0] == "b" else z) >> part[1]) & 1

    bit = jnp.where(b & 1 == 1, value(step[1]), value(step[0]))
    return bit.astype(jnp.int32).reshape(1)


def add_small_kernel(mine, got, out):
    out[...] = mine[...] + got[...]


class SmallSum:
    def __init__(self, order, sizes, array):
        self.order, self.sizes, self.array = order, sizes, array
        self.steps = halving_steps(sizes)
        self.at = -1
        self.send()

    def send(self):
        self.at += 1
        if self.at < len(self.steps):
            self.got = move(self.array, self.sizes, step_partner(self.steps[self.at]))

    def ready(self):
        return self.at == len(self.steps)

    def advance(self):
        self.array = self.order.run(
            add_small_kernel,
            [self.array, self.got],
            [whole(self.array, 1), whole(self.array, 1)],
            pl.BlockSpec(self.array.shape, lambda i: (0, 0)),
            jax.ShapeDtypeStruct(self.array.shape, f32),
            (1,),
            8,
            "add_small",
        )
        self.send()


class Sum:
    def __init__(self, order, sizes, send, keep):
        self.order, self.sizes = order, sizes
        self.steps = halving_steps(sizes)
        self.bits = [own_bit(step) for step in self.steps]
        self.at, self.down = 0, True
        self.part, self.got = keep, self.swap(send, 0)

    def swap(self, array, at):
        return move(array, self.sizes, step_partner(self.steps[at]))

    def ready(self):
        return not self.down and self.at == 1

    def advance(self):
        if not self.down:
            self.part = pair(self.order, self.part, self.got, self.bits[self.at])
            self.at -= 1
        elif self.at + 1 < len(self.steps):
            self.at += 1
            send, self.part = add_halves(self.order, self.part, self.got, self.bits[self.at])
            self.got = self.swap(send, self.at)
            return
        else:
            self.part = add_last(self.order, self.part, self.got)
            self.down = False
        self.got = self.swap(self.part, self.at)

    def send_far(self):
        self.far = self.swap(self.part, 0)

    def pieces(self):
        self.got = hold(self.order, self.got)
        return [self.part, self.got, self.far, self.swap(self.got, 0)]

    def where(self):
        other = own_bit([half[::-1] for half in self.steps][1])
        core, bit = self.bits[0], self.bits[1]
        half, far = core * 2, (1 - core) * 2
        return jnp.concatenate([half + bit, half + 1 - bit, far + other, far + 1 - other])


def per_device(
    hidden_in,
    lengths,
    qkv_weight,
    qv_bias,
    out_weight,
    out_bias,
    attn_gain,
    attn_shift,
    up_weight,
    up_bias,
    down_weight,
    down_bias,
    ffn_gain,
    ffn_shift,
    head_weight,
    head_bias,
    hidden_cot,
    term_cot,
):
    row_count, seg_len, width = hidden_in.shape
    hidden = up_weight.shape[1]
    parts = hidden // width
    sizes = (lax.axis_size("batch"), lax.axis_size("blk"))
    nz = sizes[1]
    own_rows = row_count // nz
    n = seg_len * nz
    rows = range(own_rows)
    core = own_bit(halving_steps(sizes)[0])
    order = Order()
    places = lax.rem(lax.axis_index("blk") + jnp.arange(nz), nz).astype(jnp.int32)

    vec = jnp.concatenate(
        [
            qv_bias,
            out_bias[None],
            attn_gain[None],
            attn_shift[None],
            down_bias[None],
            ffn_gain[None],
            ffn_shift[None],
            head_weight[None],
            jnp.broadcast_to(head_bias[None], (1, width)),
            up_bias.reshape(parts, width),
            jnp.zeros((-(V_UP + parts) % 8, width), bf16),
        ],
        axis=0,
    ).astype(f32)
    high = term_cot.astype(bf16)
    rest = (term_cot - high.astype(f32)).astype(bf16)
    terms = jnp.pad(jnp.stack([high, rest], axis=1), ((0, 0), (0, PACK - 2), (0, width - seg_len)))
    packed_cot = jnp.concatenate([hidden_cot, terms], axis=1)

    blocks = []
    for r in rows:
        got = send_round(pick(order, hidden_in, places, r, 1), sizes, 1)
        got[1] = hold(order, got[1])
        blocks.append([b[0] for b in got])
    held = ()
    for r in rows:
        held = attend(order, blocks[r], lengths, qkv_weight, vec, own_rows, r, held)
        if r == 0:
            cots = send_round(pick(order, packed_cot, places, 0, own_rows), sizes, 1)
    x, q, k, v, att, probs = held
    act, slope, low, n1, n2, stats, *hid = feed(
        order, x, att, out_weight, up_weight, down_weight, vec, nz, own_rows
    )
    outs = send_round(hid, sizes, -1)
    fg, head_sums = head_back(order, cots, n2, stats, vec)
    d_send = weight_rows(order, act, fg, 1 - core, 384)
    d = Sum(order, sizes, d_send, weight_rows(order, act, fg, core, 384))
    d.advance()
    gate_grad, ag, feed_sums = feed_back(
        order, fg, slope, n1, stats, up_weight, down_weight, vec, n // 2
    )
    d.advance()
    hidden_out, term_weight = place(
        order, outs, places, own_rows, seg_len, bf16, with_term=True
    )
    up_args = (low, att, gate_grad, ag)
    u_send = weight_up(order, *up_args, 1 - core)
    u = Sum(order, sizes, u_send, weight_up(order, *up_args, core))
    u.advance()
    d.advance()
    held, grads = (), []
    for r in rows:
        *held, b0, b1, b2, b3 = attend_back(
            order, ag, out_weight, q, k, v, att, probs, qkv_weight, nz, own_rows, r, held
        )
        if r == 0:
            d.advance()
        u.advance()
        grads.append(send_round([b0, b1, b2, b3], sizes, -1))
    proj_grad, qv_sums = held
    grad_hidden = place(order, grads[0], places, own_rows, seg_len, f32)
    q_send = weight_qkv(order, x, proj_grad, 1 - core)
    q = Sum(order, sizes, q_send, weight_qkv(order, x, proj_grad, core))
    where = q.where()
    q.advance()
    u.advance()
    for r in rows[1:]:
        grad_hidden = place(order, grads[r], places, own_rows, seg_len, f32, r, grad_hidden)
    (grad_hidden,) = grad_hidden
    d.advance()
    small = SmallSum(order, sizes, jnp.concatenate([head_sums, feed_sums, qv_sums], axis=0))
    q.advance()
    u.advance()
    small.advance()
    q.advance()
    d.advance()
    small.advance()
    u.advance()
    q.advance()
    small.advance()
    d.advance()
    small.advance()
    q.advance()
    u.advance()
    while not small.ready():
        small.advance()
    while not d.ready():
        d.advance()
    d.send_far()
    q.advance()
    while not u.ready():
        u.advance()
    u.send_far()
    d_pieces = d.pieces()
    q.advance()
    grad_down = join_rows(order, d_pieces, where)
    while not q.ready():
        q.advance()
    q.send_far()
    grad_up, grad_out = join_columns(order, u.pieces(), where, hidden, width)
    early, late = small.array[0:16], small.array[16:]
    grad_qv = sum(late[8 * r : 8 * r + 2] for r in rows)
    vectors = [early[i] for i in (10, 8, 9)]
    vectors += [early[11 : 11 + parts].reshape(hidden)]
    vectors += [early[i] for i in (3, 0, 1, 2)] + [early[4, 0:1]]
    (grad_qkv,) = join_columns(order, q.pieces(), where, 3 * width)
    return (
        hidden_out.reshape(hidden_in.shape),
        term_weight.reshape(row_count, seg_len),
        grad_hidden.reshape(hidden_in.shape),
        grad_qkv,
        grad_qv,
        grad_out,
        vectors[0],
        vectors[1],
        vectors[2],
        grad_up,
        vectors[3],
        grad_down,
        vectors[4],
        vectors[5],
        vectors[6],
        vectors[7],
        vectors[8],
    )


def solution(mesh):
    split = P("batch", "blk", None)
    flat = P("batch", "blk")
    return jax.shard_map(
        per_device,
        mesh=mesh,
        in_specs=(split, P("batch", None)) + (P(),) * 14 + (split, flat),
        out_specs=(split, flat, split) + (P(),) * 14,
        check_vma=False,
    )
```
